32 devices in a mesh: lon: 8 (over y, x, core), lat: 4 (over z).
Axes of the slice: x: 2, y: 2, z: 4, core: 2. Of those that a mesh axis runs over, the one named last changes fastest.
Arguments:
- members: bfloat16 [80, 2, 128, 1024], P(None, None, 'lat', 'lon'), may hold values from -18 to 18
- gradient: float32 [2, 128, 1024], P(None, 'lat', 'lon'), may hold values from -6 to 6
- lon_taper: bfloat16 [513], replicated, as said below
- lat_taper: bfloat16 [129], replicated, as said below
Outputs:
- covariance_product: float32 [2, 128, 1024], P(None, 'lat', 'lon')
The draws below stay inside these ranges and needn't reach their ends.
Inputs may be any that keep to these rules, and one draw needn't show every extreme that they name: lon_taper holds the weights of offsets -256 to 256 in that order; none is negative. lat_taper holds the weights of offsets -64 to 64 in that order; none is negative.
All inputs are finite; a program needn't handle non-finite values.
Results may differ from the reference program's by a relative error of at most 0.0041.
Values may be sent and summed in bfloat16 or wider, within the bound.
A program may use at most 64 MiB of HBM per device.

```python
import math
import jax
import jax.numpy as jnp
from jax import lax

MEMBERS = 80
LEV = 2
CLON = 128
CLAT = 32
NLON = 1024
NLAT = 128


def rough_taper(key, half, lower, span):
    dist = jnp.arange(-half, half + 1).astype(jnp.float32)
    envelope = jnp.cos(dist * (math.pi / (2 * half + 2))) ** 2 / math.sqrt(0.75 * (half + 1))
    factor = lower + span * jax.random.uniform(key, (2 * half + 1,), jnp.float32)
    return envelope * factor


def draw_lon_taper(key, part):
    key = jax.random.fold_in(key, 11)
    return rough_taper(key, 2 * CLON, 0.4, 1.2).astype(jnp.bfloat16)


def draw_lat_taper(key, part):
    key = jax.random.fold_in(key, 12)
    return rough_taper(key, 2 * CLAT, 0.4, 1.2).astype(jnp.bfloat16)


def block_scale(key, extent, pieces, smallest, high):
    loudness, own = 1.0, jax.random.fold_in(key, 6)
    for position, parts in pieces:
        heights = jnp.exp(jax.random.uniform(jax.random.fold_in(own, position), (parts,), jnp.float32, smallest / len(pieces), high / len(pieces)))
        loudness = loudness * jnp.repeat(heights, extent[position] // parts).reshape([-1 if axis == position else 1 for axis in range(len(extent))])
    return loudness


def scatter_about(stream_key, dims, scale, bound, cuts=(), kind=jnp.bfloat16):
    values = jax.random.normal(stream_key, dims, jnp.float32) * scale
    if len(cuts) > 0:
        values = block_scale(stream_key, dims, cuts, -0.22, 0.18) * values
    return jnp.clip(values, min=-bound, max=bound).astype(kind)


def setup_inputs(seed: int = 0) -> dict:
    splits = jax.random.split(jax.random.key(seed), 5)
    return {
        "members": scatter_about(splits[0], (MEMBERS, LEV, NLAT, NLON), 3.0, 18.0, ((2, 4), (3, 8))),
        "gradient": scatter_about(splits[1], (LEV, NLAT, NLON), 1.0, 6.0, ((1, 4), (2, 8)), jnp.float32),
        "lon_taper": draw_lon_taper(jax.random.fold_in(splits[4], 71), 0),
        "lat_taper": draw_lat_taper(jax.random.fold_in(splits[4], 71), 0),
    }


def taper_kernel(weights, half, length):
    where_at = (jnp.arange(-half, half + 1) % length).astype(jnp.int32)
    return jnp.zeros((length,), jnp.float32).at[where_at].set(weights.astype(jnp.float32))


def reference(members, gradient, lon_taper, lat_taper):
    spec_lon = jnp.fft.rfft(taper_kernel(lon_taper, 2 * CLON, NLON))
    padded_len = NLAT + 4 * CLAT
    spec_lat = jnp.fft.rfft(taper_kernel(lat_taper, 2 * CLAT, padded_len))[:, None]

    def one_member(total, member):
        product = (member.astype(jnp.float32) * gradient).astype(jnp.bfloat16)
        product = lax.optimization_barrier(product).astype(jnp.float32)
        along_lon = jnp.fft.irfft(jnp.fft.rfft(product, axis=-1) * spec_lon, n=NLON, axis=-1)
        along_lon = lax.optimization_barrier(along_lon.astype(jnp.bfloat16)).astype(jnp.float32)
        along_lat = jnp.fft.irfft(jnp.fft.rfft(along_lon, n=padded_len, axis=-2) * spec_lat, n=padded_len, axis=-2)
        along_lat = along_lat[:, :NLAT, :]
        return total + member.astype(jnp.float32) * along_lat, None

    total, unused = lax.scan(one_member, jnp.zeros(gradient.shape, jnp.float32), members)
    return total / (MEMBERS - 1)
```

```python
import functools

import jax
import jax.numpy as jnp
from jax import lax
from jax.experimental import pallas as pl
from jax.experimental.pallas import tpu as pltpu
from jax.sharding import PartitionSpec as P

MESH = pl.DeviceIdType.MESH


def from_behind(value, axis, steps):
    count = lax.axis_size(axis)
    pairs = [(source, (source + steps) % count) for source in range(count)]
    return lax.ppermute(value, axis, pairs)


def from_behind_2(block, axis, distance):
    devices = range(lax.axis_size(axis))
    route = [(i - distance, i) for i in devices if i - distance in devices]
    return lax.ppermute(block, axis, route)


def taper_table(weights, block_cells):
    half = 2 * block_cells
    rows_at = jnp.arange(5 * block_cells, dtype=jnp.int32)[:, None]
    cols_at = jnp.arange(block_cells, dtype=jnp.int32)[None, :]
    dist = cols_at + half - rows_at
    where_at = jnp.clip(dist + half, 0, 2 * half)
    picked = jnp.take(weights, where_at, axis=0)
    return jnp.where(jnp.abs(dist) <= half, picked, jnp.zeros_like(picked))


def cycle_blocks(values):
    pieces = {}
    for offset in (2, 1, -1, -2):
        pieces[offset] = from_behind(values, "lon", offset)
    return jnp.concatenate([pieces[2], pieces[1], values, pieces[-1], pieces[-2]], axis=3)


def line_blocks(values):
    pieces = {}
    for offset in (2, 1, -1, -2):
        pieces[offset] = from_behind_2(values, "lat", offset)
    return jnp.concatenate([pieces[2], pieces[1], values, pieces[-1], pieces[-2]], axis=2)


def halo_plan(members, gradient, lon_taper, lat_taper):
    clat = gradient.shape[1]
    clon = gradient.shape[2]
    count = members.shape[0]
    products = (members.astype(jnp.float32) * gradient).astype(jnp.bfloat16)
    lon_table = taper_table(lon_taper, clon)
    extended = cycle_blocks(products)
    along_lon = jnp.einsum(
        "mlae,ei->mlai", extended, lon_table, preferred_element_type=jnp.float32
    ).astype(jnp.bfloat16)
    lat_table = taper_table(lat_taper, clat)
    rimmed = line_blocks(along_lon)
    along_lat = jnp.einsum("mlec,ea->mlac", rimmed, lat_table, preferred_element_type=jnp.float32)
    weighted = jnp.sum(members.astype(jnp.float32) * along_lat, axis=0)
    return weighted / (count - 1)


def member_kernel(
    n_lon, n_lat, count,
    members, gradient, lon_line, lat_line, out,
    grad_z, grad_all, taken, wide, lon_table, lat_table, partial, parts,
    gz_send, gz_recv, ga_send, ga_recv, m_send, m_recv, r_send, r_recv, own_sem,
):
    i, j = lax.axis_index("lon"), lax.axis_index("lat")
    clat, clon = gradient.shape[1], gradient.shape[2]
    n = n_lon * n_lat
    share = taken.shape[1]
    lat_cells = n_lat * clat
    me = i * n_lat + j
    level = lax.rem(i, 2)

    def shares_of(i_to, j_to):
        return ((i_to // 2) * n_lat + j_to) * share

    def other(k):
        i_to = lax.rem(i + k // n_lat, n_lon)
        j_to = lax.rem(j + lax.rem(k, n_lat), n_lat)
        return i_to, j_to

    barrier = pltpu.get_barrier_semaphore()

    def greet(k, c):
        i_to, j_to = other(k)
        pl.semaphore_signal(barrier, inc=1, device_id={"lon": i_to, "lat": j_to}, device_id_type=MESH)
        return c

    lax.fori_loop(1, n, greet, 0)
    pl.semaphore_wait(barrier, n - 1)

    def grad_z_copy(k):
        j_to = lax.rem(j + k, n_lat)
        return pltpu.make_async_remote_copy(
            src_ref=gradient, dst_ref=grad_z.at[j],
            send_sem=gz_send.at[j_to], recv_sem=gz_recv.at[j],
            device_id={"lon": i, "lat": j_to}, device_id_type=MESH,
        )

    for k in range(1, n_lat):
        grad_z_copy(k).start()

    def member_copy(k):
        i_to, j_to = other(k)
        return pltpu.make_async_remote_copy(
            src_ref=members.at[pl.ds(shares_of(i_to, j_to), share), lax.rem(i_to, 2)],
            dst_ref=taken.at[i, :, pl.ds(pl.multiple_of(j * clat, clat), clat), :],
            send_sem=m_send.at[i_to * n_lat + j_to], recv_sem=m_recv.at[me],
            device_id={"lon": i_to, "lat": j_to}, device_id_type=MESH,
        )

    def start_members(k, c):
        member_copy(k).start()
        return c

    lax.fori_loop(1, n, start_members, 0)
    own = pltpu.make_async_copy(
        members.at[pl.ds(shares_of(i, j), share), level],
        taken.at[i, :, pl.ds(pl.multiple_of(j * clat, clat), clat), :],
        own_sem,
    )
    own.start()
    grad_z[j] = gradient[...]

    for k in range(1, n_lat):
        j_from = lax.rem(j + k, n_lat)
        pltpu.make_async_remote_copy(
            src_ref=gradient, dst_ref=grad_z.at[j_from],
            send_sem=gz_send.at[j_from], recv_sem=gz_recv.at[j_from],
            device_id={"lon": i, "lat": j_from}, device_id_type=MESH,
        ).wait()

    def grad_all_copy(k):
        i_to = lax.rem(i + k, n_lon)
        return pltpu.make_async_remote_copy(
            src_ref=grad_z.at[:, lax.rem(i_to, 2)], dst_ref=grad_all.at[i],
            send_sem=ga_send.at[i_to], recv_sem=ga_recv.at[i],
            device_id={"lon": i_to, "lat": j}, device_id_type=MESH,
        )

    for k in range(1, n_lon):
        grad_all_copy(k).start()
    grad_all[i] = grad_z[:, level]

    rows, cols = lon_table.shape
    line = lon_line.shape[1]
    spread = jnp.broadcast_to(lon_line[...], (rows, line))
    turned = pltpu.roll(spread, line - 4 * clon - 2 * clon, 1, stride=1, stride_axis=0)
    lon_table[...] = turned[:, :cols].astype(jnp.bfloat16)
    spread = jnp.broadcast_to(lat_line[...], (lat_cells, lat_line.shape[1]))
    turned = pltpu.roll(spread, lat_line.shape[1] - lat_cells, 1, stride=1, stride_axis=0)
    lat_table[...] = turned[:, :lat_cells].astype(jnp.bfloat16)

    for k in range(1, n_lon):
        i_from = lax.rem(i + k, n_lon)
        pltpu.make_async_remote_copy(
            src_ref=grad_z.at[:, 0], dst_ref=grad_all.at[i_from],
            send_sem=ga_send.at[i_from], recv_sem=ga_recv.at[i_from],
            device_id={"lon": i_from, "lat": j}, device_id_type=MESH,
        ).wait()

    own.wait()

    def wait_members(k, c):
        i_from, j_from = other(k)
        s = i_from * n_lat + j_from
        pltpu.make_async_remote_copy(
            src_ref=members.at[pl.ds(0, share), 0],
            dst_ref=taken.at[i_from, :, pl.ds(pl.multiple_of(j_from * clat, clat), clat), :],
            send_sem=m_send.at[s], recv_sem=m_recv.at[s],
            device_id={"lon": i_from, "lat": j_from}, device_id_type=MESH,
        ).wait()
        return c

    lax.fori_loop(1, n, wait_members, 0)

    for b in range(n_lon):
        g = grad_all[b].reshape(lat_cells, clon)
        p = (taken[b].astype(jnp.float32) * g[None]).astype(jnp.bfloat16)
        p = p.reshape(share * lat_cells, clon)
        for at in (b - n_lon + 2, b + 2, b + n_lon + 2):
            if 0 <= at < n_lon + 4:
                wide[:, at * clon:(at + 1) * clon] = p

    for o in range(n_lon // 2):
        along_lon = jnp.dot(
            wide[:, 2 * o * clon:(2 * o + 6) * clon], lon_table[...],
            preferred_element_type=jnp.float32,
        ).astype(jnp.bfloat16)
        total = jnp.zeros((lat_cells, 2 * clon), jnp.float32)
        for m in range(share):
            along_lat = jnp.dot(
                lat_table[...], along_lon[m * lat_cells:(m + 1) * lat_cells],
                preferred_element_type=jnp.float32,
            )
            x = jnp.concatenate([taken[2 * o, m], taken[2 * o + 1, m]], axis=1)
            total += x.astype(jnp.float32) * along_lat
        partial[2 * o] = total[:, :clon].astype(jnp.bfloat16)
        partial[2 * o + 1] = total[:, clon:].astype(jnp.bfloat16)

    def part_copy(k):
        i_to, j_to = other(k)
        return pltpu.make_async_remote_copy(
            src_ref=partial.at[i_to, pl.ds(pl.multiple_of(j_to * clat, clat), clat), :],
            dst_ref=parts.at[level, (i // 2) * n_lat + j],
            send_sem=r_send.at[i_to * n_lat + j_to], recv_sem=r_recv.at[me],
            device_id={"lon": i_to, "lat": j_to}, device_id_type=MESH,
        )

    def start_parts(k, c):
        part_copy(k).start()
        return c

    lax.fori_loop(1, n, start_parts, 0)
    parts[level, (i // 2) * n_lat + j] = partial[i, pl.ds(pl.multiple_of(j * clat, clat), clat), :]

    def wait_parts(k, c):
        i_from, j_from = other(k)
        s = i_from * n_lat + j_from
        pltpu.make_async_remote_copy(
            src_ref=partial.at[i_from, pl.ds(pl.multiple_of(j_from * clat, clat), clat), :],
            dst_ref=parts.at[lax.rem(i_from, 2), (i_from // 2) * n_lat + j_from],
            send_sem=r_send.at[s], recv_sem=r_recv.at[s],
            device_id={"lon": i_from, "lat": j_from}, device_id_type=MESH,
        ).wait()
        return c

    lax.fori_loop(1, n, wait_parts, 0)
    for l in range(2):
        out[l] = jnp.sum(parts[l].astype(jnp.float32), axis=0) / (count - 1)


def member_plan(members, gradient, lon_taper, lat_taper):
    n_lon, n_lat = lax.axis_size("lon"), lax.axis_size("lat")
    count, levels, clat, clon = members.shape
    share = count // (n_lon // 2 * n_lat)
    lat_cells = n_lat * clat
    line = 8 * clon
    lon_line = jnp.pad(lon_taper.astype(jnp.float32), (2 * clon, line - 6 * clon - 1))[None]
    side = lat_cells - 2 * clat
    lat_line = jnp.pad(lat_taper[::-1].astype(jnp.float32), (side, side - 1))[None]
    n = n_lon * n_lat
    vmem = pl.BlockSpec(memory_space=pltpu.VMEM)
    dma = pltpu.SemaphoreType.DMA
    return pl.pallas_call(
        functools.partial(member_kernel, n_lon, n_lat, count),
        out_shape=jax.ShapeDtypeStruct(gradient.shape, jnp.float32),
        in_specs=[pl.BlockSpec(memory_space=pl.ANY), vmem, vmem, vmem],
        out_specs=vmem,
        scratch_shapes=[
            pltpu.VMEM((n_lat, levels, clat, clon), jnp.float32),
            pltpu.VMEM((n_lon, n_lat, clat, clon), jnp.float32),
            pltpu.VMEM((n_lon, share, lat_cells, clon), jnp.bfloat16),
            pltpu.VMEM((share * lat_cells, (n_lon + 4) * clon), jnp.bfloat16),
            pltpu.VMEM((6 * clon, 2 * clon), jnp.bfloat16),
            pltpu.VMEM((lat_cells, lat_cells), jnp.bfloat16),
            pltpu.VMEM((n_lon, lat_cells, clon), jnp.bfloat16),
            pltpu.VMEM((2, n // 2, clat, clon), jnp.bfloat16),
            dma((n_lat,)), dma((n_lat,)), dma((n_lon,)), dma((n_lon,)),
            dma((n,)), dma((n,)), dma((n,)), dma((n,)), dma,
        ],
        compiler_params=pltpu.CompilerParams(
            collective_id=0, has_side_effects=True, vmem_limit_bytes=40 * 1024 * 1024
        ),
    )(members, gradient, lon_line, lat_line)


def per_device(members, gradient, lon_taper, lat_taper):
    n_lon, n_lat = lax.axis_size("lon"), lax.axis_size("lat")
    count, levels, clat, clon = members.shape
    even = levels == 2 and n_lon % 2 == 0 and n_lon >= 6
    if even and count % (n_lon // 2 * n_lat) == 0 and n_lat * clat % 128 == 0 and n_lat >= 3:
        return member_plan(members, gradient, lon_taper, lat_taper)
    return halo_plan(members, gradient, lon_taper, lat_taper)


def solution(mesh):
    in_specs = (P(None, None, "lat", "lon"), P(None, "lat", "lon"), P(), P())
    out_specs = P(None, "lat", "lon")
    return jax.shard_map(
        per_device, mesh=mesh, in_specs=in_specs, out_specs=out_specs, check_vma=False
    )
```

```python
import functools

import jax
import jax.numpy as jnp
from jax import lax
from jax.experimental import pallas as pl
from jax.experimental.pallas import tpu as pltpu
from jax.sharding import PartitionSpec as P

MESH = pl.DeviceIdType.MESH
VMEM_BYTES = 60 * 1024 * 1024


def from_behind(value, axis, steps):
    count = lax.axis_size(axis)
    pairs = [(source, (source + steps) % count) for source in range(count)]
    return lax.ppermute(value, axis, pairs)


def from_behind_2(block, axis, distance):
    devices = range(lax.axis_size(axis))
    route = [(i - distance, i) for i in devices if i - distance in devices]
    return lax.ppermute(block, axis, route)


def taper_table(weights, block_cells):
    half = 2 * block_cells
    rows_at = jnp.arange(5 * block_cells, dtype=jnp.int32)[:, None]
    cols_at = jnp.arange(block_cells, dtype=jnp.int32)[None, :]
    dist = cols_at + half - rows_at
    where_at = jnp.clip(dist + half, 0, 2 * half)
    picked = jnp.take(weights, where_at, axis=0)
    return jnp.where(jnp.abs(dist) <= half, picked, jnp.zeros_like(picked))


def cycle_blocks(values):
    pieces = {}
    for offset in (2, 1, -1, -2):
        pieces[offset] = from_behind(values, "lon", offset)
    return jnp.concatenate([pieces[2], pieces[1], values, pieces[-1], pieces[-2]], axis=3)


def line_blocks(values):
    pieces = {}
    for offset in (2, 1, -1, -2):
        pieces[offset] = from_behind_2(values, "lat", offset)
    return jnp.concatenate([pieces[2], pieces[1], values, pieces[-1], pieces[-2]], axis=2)


def halo_plan(members, gradient, lon_taper, lat_taper):
    clat = gradient.shape[1]
    clon = gradient.shape[2]
    count = members.shape[0]
    products = (members.astype(jnp.float32) * gradient).astype(jnp.bfloat16)
    lon_table = taper_table(lon_taper, clon)
    extended = cycle_blocks(products)
    along_lon = jnp.einsum(
        "mlae,ei->mlai", extended, lon_table, preferred_element_type=jnp.float32
    ).astype(jnp.bfloat16)
    lat_table = taper_table(lat_taper, clat)
    rimmed = line_blocks(along_lon)
    along_lat = jnp.einsum("mlec,ea->mlac", rimmed, lat_table, preferred_element_type=jnp.float32)
    weighted = jnp.sum(members.astype(jnp.float32) * along_lat, axis=0)
    return weighted / (count - 1)


def member_kernel(
    n_lon, n_lat, count,
    members, gradient, lines, out,
    grad_z, grad_all, taken, stack, along, total, lon_table, lat_table, partial, parts,
    gz_send, gz_recv, own_grad, ga_send, ga_recv, m_send, m_recv, r_send, r_recv,
):
    i, j = lax.axis_index("lon"), lax.axis_index("lat")
    clat, clon = gradient.shape[1], gradient.shape[2]
    n = n_lon * n_lat
    share = taken.shape[0]
    lat_cells = n_lat * clat
    pairs = n_lon // 2
    level = lax.rem(i, 2)
    place = (i // 2) * n_lat + j

    def other(k):
        i_to = lax.rem(i + k // n_lat, n_lon)
        j_to = lax.rem(j + lax.rem(k, n_lat), n_lat)
        return i_to, j_to

    def lat_rows(j_at):
        return pl.ds(pl.multiple_of(j_at * clat, clat), clat)

    barrier = pltpu.get_barrier_semaphore()

    def greet(k, c):
        i_to, j_to = other(k)
        pl.semaphore_signal(barrier, inc=1, device_id={"lon": i_to, "lat": j_to}, device_id_type=MESH)
        return c

    lax.fori_loop(1, n, greet, 0)

    own = pltpu.make_async_copy(gradient, grad_z.at[j], own_grad)
    own.start()
    for m in range(share):
        pltpu.make_async_copy(
            members.at[place * share + m, level], taken.at[m, i, lat_rows(j), :], m_recv.at[m]
        ).start()

    rows, cols = lon_table.shape
    line = 8 * clon
    spread = jnp.broadcast_to(lines[:, :line], (rows, line))
    turned = pltpu.roll(spread, line - 6 * clon, 1, stride=1, stride_axis=0)
    lon_table[...] = turned[:, :cols].astype(jnp.bfloat16)
    spread = jnp.broadcast_to(lines[:, line:], (lat_cells, 2 * lat_cells))
    turned = pltpu.roll(spread, lat_cells, 1, stride=1, stride_axis=0)
    lat_table[...] = turned[:, :lat_cells].T.astype(jnp.bfloat16)

    pl.semaphore_wait(barrier, n - 1)
    own.wait()

    def grad_z_copies(s):
        up = pltpu.make_async_remote_copy(
            src_ref=grad_z.at[lax.max(j - s, 0)], dst_ref=grad_z.at[lax.max(j - s, 0)],
            send_sem=gz_send.at[0, s], recv_sem=gz_recv.at[0, s],
            device_id={"lon": i, "lat": lax.min(j + 1, n_lat - 1)}, device_id_type=MESH,
        )
        down = pltpu.make_async_remote_copy(
            src_ref=grad_z.at[lax.min(j + s, n_lat - 1)], dst_ref=grad_z.at[lax.min(j + s, n_lat - 1)],
            send_sem=gz_send.at[1, s], recv_sem=gz_recv.at[1, s],
            device_id={"lon": i, "lat": lax.max(j - 1, 0)}, device_id_type=MESH,
        )
        return up, down

    def grad_z_start(s):
        up, down = grad_z_copies(s)

        @pl.when((j - s >= 0) & (j + 1 < n_lat))
        def _():
            up.start()

        @pl.when((j + s < n_lat) & (j - 1 >= 0))
        def _():
            down.start()

    def grad_z_wait(s):
        up, down = grad_z_copies(s)

        @pl.when((j - s >= 0) & (j + 1 < n_lat))
        def _():
            up.wait_send()

        @pl.when((j + s < n_lat) & (j - 1 >= 0))
        def _():
            down.wait_send()

        @pl.when(j - 1 - s >= 0)
        def _():
            pltpu.make_async_remote_copy(
                src_ref=grad_z.at[0], dst_ref=grad_z.at[lax.max(j - 1 - s, 0)],
                send_sem=gz_send.at[0, s], recv_sem=gz_recv.at[0, s],
                device_id={"lon": i, "lat": lax.max(j - 1, 0)}, device_id_type=MESH,
            ).wait_recv()

        @pl.when(j + 1 + s < n_lat)
        def _():
            pltpu.make_async_remote_copy(
                src_ref=grad_z.at[0], dst_ref=grad_z.at[lax.min(j + 1 + s, n_lat - 1)],
                send_sem=gz_send.at[1, s], recv_sem=gz_recv.at[1, s],
                device_id={"lon": i, "lat": lax.min(j + 1, n_lat - 1)}, device_id_type=MESH,
            ).wait_recv()

    def start_members(m):
        def start(k, c):
            i_to, j_to = other(k)
            at = ((i_to // 2) * n_lat + j_to) * share + m
            pltpu.make_async_remote_copy(
                src_ref=members.at[at, lax.rem(i_to, 2)], dst_ref=taken.at[m, i, lat_rows(j), :],
                send_sem=m_send.at[m], recv_sem=m_recv.at[m],
                device_id={"lon": i_to, "lat": j_to}, device_id_type=MESH,
            ).start()
            return c

        lax.fori_loop(1, n, start, 0)

    sent = members.at[pl.ds(0, n - 1), 0]

    def wait_members(m):
        pltpu.make_async_copy(taken.at[m], taken.at[m], m_recv.at[m]).wait()
        pltpu.make_async_copy(sent, sent, m_send.at[m]).wait()

    def grad_all_copy(k):
        i_to = lax.rem(i + k, n_lon)
        return pltpu.make_async_remote_copy(
            src_ref=grad_z.at[:, lax.rem(i_to, 2)], dst_ref=grad_all.at[i],
            send_sem=ga_send.at[i_to], recv_sem=ga_recv.at[i],
            device_id={"lon": i_to, "lat": j}, device_id_type=MESH,
        )

    grad_z_start(0)
    started = 0
    for s in range(n_lat - 1):
        if started < share:
            start_members(started)
            started += 1
        grad_z_wait(s)
        if s + 1 < n_lat - 1:
            grad_z_start(s + 1)
    for k in range(1, n_lon):
        grad_all_copy(k).start()
    for m in range(started, share):
        start_members(m)
    grad_all[i] = grad_z[:, level]
    for k in range(1, n_lon):
        i_from = lax.rem(i + k, n_lon)
        pltpu.make_async_remote_copy(
            src_ref=grad_z.at[:, 0], dst_ref=grad_all.at[i_from],
            send_sem=ga_send.at[i_from], recv_sem=ga_recv.at[i_from],
            device_id={"lon": i_from, "lat": j}, device_id_type=MESH,
        ).wait()

    def pair_term(m, o, along_lon):
        along_lat = jnp.dot(lat_table[...], along_lon, preferred_element_type=jnp.float32)
        x = jnp.concatenate([taken[m, 2 * o], taken[m, 2 * o + 1]], axis=1)
        return x.astype(jnp.float32) * along_lat

    def part_copy(i_to, j_to):
        return pltpu.make_async_remote_copy(
            src_ref=partial.at[i_to, lat_rows(j_to), :], dst_ref=parts.at[level, place],
            send_sem=r_send, recv_sem=r_recv,
            device_id={"lon": i_to, "lat": j_to}, device_id_type=MESH,
        )

    for m in range(share):
        wait_members(m)
        for b in range(n_lon):
            g = grad_all[b].reshape(lat_cells, clon)
            p = (taken[m, b].astype(jnp.float32) * g).astype(jnp.bfloat16)
            for step in (-1, 0, 1):
                o = (b // 2 + step) % pairs
                at = (b % 2 + 2 - 2 * step) * clon
                stack[o * lat_cells:(o + 1) * lat_cells, at:at + clon] = p
        along_lon = jnp.dot(
            stack[...], lon_table[...], preferred_element_type=jnp.float32
        ).astype(jnp.bfloat16)
        if m < share - 1:
            for o in range(pairs):
                term = pair_term(m, o, along_lon[o * lat_cells:(o + 1) * lat_cells])
                total[o] = term if m == 0 else total[o] + term
            continue
        along[...] = along_lon
        for t in range(pairs):
            o = lax.rem(i // 2 + 1 + t, pairs)
            window = along[pl.ds(pl.multiple_of(o * lat_cells, lat_cells), lat_cells), :]
            done = pair_term(m, o, window)
            if share > 1:
                done += total[o]
            for c in range(2):
                partial[2 * o + c] = done[:, c * clon:(c + 1) * clon].astype(jnp.bfloat16)
            for c in range(2):
                for k in range(n_lat):
                    j_to = lax.rem(j + 1 + k, n_lat)
                    if t < pairs - 1 or k < n_lat - 1:
                        part_copy(2 * o + c, j_to).start()
                    else:
                        @pl.when(c != level)
                        def _():
                            part_copy(2 * o + c, j_to).start()

    kept = pltpu.make_async_copy(partial.at[i, lat_rows(j), :], parts.at[level, place], r_recv)
    kept.start()
    pltpu.make_async_copy(parts, parts, r_recv).wait()
    for l in range(2):
        out[l] = jnp.sum(parts[l].astype(jnp.float32), axis=0) / (count - 1)
    pltpu.make_async_copy(sent, sent, r_send).wait()


def member_plan(members, gradient, lon_taper, lat_taper):
    n_lon, n_lat = lax.axis_size("lon"), lax.axis_size("lat")
    count, levels, clat, clon = members.shape
    share = count // (n_lon // 2 * n_lat)
    lat_cells = n_lat * clat
    side = lat_cells - 2 * clat
    lines = jnp.concatenate([
        jnp.pad(lon_taper, (2 * clon, 2 * clon - 1)), jnp.pad(lat_taper, (side, side - 1))
    ]).astype(jnp.float32)[None]
    n = n_lon * n_lat
    vmem = pl.BlockSpec(memory_space=pltpu.VMEM)
    hbm = pl.BlockSpec(memory_space=pl.ANY)
    dma = pltpu.SemaphoreType.DMA
    return pl.pallas_call(
        functools.partial(member_kernel, n_lon, n_lat, count),
        out_shape=jax.ShapeDtypeStruct(gradient.shape, jnp.float32),
        in_specs=[hbm, hbm, vmem],
        out_specs=vmem,
        scratch_shapes=[
            pltpu.VMEM((n_lat, levels, clat, clon), jnp.float32),
            pltpu.VMEM((n_lon, n_lat, clat, clon), jnp.float32),
            pltpu.VMEM((share, n_lon, lat_cells, clon), jnp.bfloat16),
            pltpu.VMEM((n_lon // 2 * lat_cells, 6 * clon), jnp.bfloat16),
            pltpu.VMEM((n_lon // 2 * lat_cells, 2 * clon), jnp.bfloat16),
            pltpu.VMEM((n_lon // 2, lat_cells, 2 * clon), jnp.float32),
            pltpu.VMEM((6 * clon, 2 * clon), jnp.bfloat16),
            pltpu.VMEM((lat_cells, lat_cells), jnp.bfloat16),
            pltpu.VMEM((n_lon, lat_cells, clon), jnp.bfloat16),
            pltpu.VMEM((2, n // 2, clat, clon), jnp.bfloat16),
            dma((2, n_lat)), dma((2, n_lat)), dma, dma((n_lon,)), dma((n_lon,)),
            dma((share,)), dma((share,)), dma, dma,
        ],
        compiler_params=pltpu.CompilerParams(
            collective_id=0, has_side_effects=True, vmem_limit_bytes=VMEM_BYTES
        ),
    )(members, gradient, lines)


def per_device(members, gradient, lon_taper, lat_taper):
    n_lon, n_lat = lax.axis_size("lon"), lax.axis_size("lat")
    count, levels, clat, clon = members.shape
    even = levels == 2 and n_lon % 2 == 0 and n_lon >= 6
    if even and count % (n_lon // 2 * n_lat) == 0 and n_lat * clat % 128 == 0 and n_lat >= 3 and count >= n_lon * n_lat:
        return member_plan(members, gradient, lon_taper, lat_taper)
    return halo_plan(members, gradient, lon_taper, lat_taper)


def solution(mesh):
    in_specs = (P(None, None, "lat", "lon"), P(None, "lat", "lon"), P(), P())
    out_specs = P(None, "lat", "lon")
    return jax.shard_map(
        per_device, mesh=mesh, in_specs=in_specs, out_specs=out_specs, check_vma=False
    )
```

```python
import functools

import jax
import jax.numpy as jnp
from jax import lax
from jax.experimental import pallas as pl
from jax.experimental.pallas import tpu as pltpu
from jax.sharding import PartitionSpec as P

MESH = pl.DeviceIdType.MESH
VMEM_BYTES = 60 * 1024 * 1024


def from_behind(value, axis, steps):
    count = lax.axis_size(axis)
    pairs = [(source, (source + steps) % count) for source in range(count)]
    return lax.ppermute(value, axis, pairs)


def from_behind_2(block, axis, distance):
    devices = range(lax.axis_size(axis))
    route = [(i - distance, i) for i in devices if i - distance in devices]
    return lax.ppermute(block, axis, route)


def taper_table(weights, block_cells):
    half = 2 * block_cells
    rows_at = jnp.arange(5 * block_cells, dtype=jnp.int32)[:, None]
    cols_at = jnp.arange(block_cells, dtype=jnp.int32)[None, :]
    dist = cols_at + half - rows_at
    where_at = jnp.clip(dist + half, 0, 2 * half)
    picked = jnp.take(weights, where_at, axis=0)
    return jnp.where(jnp.abs(dist) <= half, picked, jnp.zeros_like(picked))


def cycle_blocks(values):
    pieces = {}
    for offset in (2, 1, -1, -2):
        pieces[offset] = from_behind(values, "lon", offset)
    return jnp.concatenate([pieces[2], pieces[1], values, pieces[-1], pieces[-2]], axis=3)


def line_blocks(values):
    pieces = {}
    for offset in (2, 1, -1, -2):
        pieces[offset] = from_behind_2(values, "lat", offset)
    return jnp.concatenate([pieces[2], pieces[1], values, pieces[-1], pieces[-2]], axis=2)


def halo_plan(members, gradient, lon_taper, lat_taper):
    clat = gradient.shape[1]
    clon = gradient.shape[2]
    count = members.shape[0]
    products = (members.astype(jnp.float32) * gradient).astype(jnp.bfloat16)
    lon_table = taper_table(lon_taper, clon)
    extended = cycle_blocks(products)
    along_lon = jnp.einsum(
        "mlae,ei->mlai", extended, lon_table, preferred_element_type=jnp.float32
    ).astype(jnp.bfloat16)
    lat_table = taper_table(lat_taper, clat)
    rimmed = line_blocks(along_lon)
    along_lat = jnp.einsum("mlec,ea->mlac", rimmed, lat_table, preferred_element_type=jnp.float32)
    weighted = jnp.sum(members.astype(jnp.float32) * along_lat, axis=0)
    return weighted / (count - 1)


def member_kernel(
    n_lon, n_lat, count,
    members, gradient, lon_taper, lat_taper, out,
    lon_line, lat_line, grad_z, grad_all, taken, stack, along, total, lon_table, lat_table, partial, parts,
    line_sem, gz_send, gz_recv, own_grad, ga_send, ga_recv, m_send, m_recv, r_send, r_recv,
):
    i, j = lax.axis_index("lon"), lax.axis_index("lat")
    clat, clon = gradient.shape[1], gradient.shape[2]
    n = n_lon * n_lat
    share = taken.shape[0]
    lat_cells = n_lat * clat
    pairs = n_lon // 2
    level = lax.rem(i, 2)
    place = (i // 2) * n_lat + j

    def other(k):
        i_to = lax.rem(i + k // n_lat, n_lon)
        j_to = lax.rem(j + lax.rem(k, n_lat), n_lat)
        return i_to, j_to

    def lat_rows(j_at):
        return pl.ds(pl.multiple_of(j_at * clat, clat), clat)

    lon_in = pltpu.make_async_copy(lon_taper, lon_line, line_sem.at[0])
    lat_in = pltpu.make_async_copy(lat_taper, lat_line, line_sem.at[1])
    lon_in.start()
    lat_in.start()

    barrier = pltpu.get_barrier_semaphore()

    def greet(k, c):
        i_to, j_to = other(k)
        pl.semaphore_signal(barrier, inc=1, device_id={"lon": i_to, "lat": j_to}, device_id_type=MESH)
        return c

    lax.fori_loop(1, n, greet, 0)

    own = pltpu.make_async_copy(gradient, grad_z.at[j], own_grad)
    own.start()
    for m in range(share):
        pltpu.make_async_copy(
            members.at[place * share + m, level], taken.at[m, i, lat_rows(j), :], m_recv.at[m]
        ).start()

    def centred(values, length):
        values = values.astype(jnp.float32).reshape(1, values.shape[0])
        side = (length - values.shape[1] + 1) // 2
        return jnp.pad(values, ((0, 0), (side, side - 1)))

    lon_in.wait()
    lat_in.wait()
    rows, cols = lon_table.shape
    line = 8 * clon
    spread = jnp.broadcast_to(centred(lon_line[...], line), (rows, line))
    turned = pltpu.roll(spread, line - 6 * clon, 1, stride=1, stride_axis=0)
    lon_table[...] = turned[:, :cols].astype(jnp.bfloat16)
    spread = jnp.broadcast_to(centred(lat_line[...], 2 * lat_cells), (lat_cells, 2 * lat_cells))
    turned = pltpu.roll(spread, lat_cells, 1, stride=1, stride_axis=0)
    lat_table[...] = turned[:, :lat_cells].T.astype(jnp.bfloat16)

    pl.semaphore_wait(barrier, n - 1)
    own.wait()

    def grad_z_copies(s):
        up = pltpu.make_async_remote_copy(
            src_ref=grad_z.at[lax.max(j - s, 0)], dst_ref=grad_z.at[lax.max(j - s, 0)],
            send_sem=gz_send.at[0, s], recv_sem=gz_recv.at[0, s],
            device_id={"lon": i, "lat": lax.min(j + 1, n_lat - 1)}, device_id_type=MESH,
        )
        down = pltpu.make_async_remote_copy(
            src_ref=grad_z.at[lax.min(j + s, n_lat - 1)], dst_ref=grad_z.at[lax.min(j + s, n_lat - 1)],
            send_sem=gz_send.at[1, s], recv_sem=gz_recv.at[1, s],
            device_id={"lon": i, "lat": lax.max(j - 1, 0)}, device_id_type=MESH,
        )
        return up, down

    def grad_z_start(s):
        up, down = grad_z_copies(s)

        @pl.when((j - s >= 0) & (j + 1 < n_lat))
        def _():
            up.start()

        @pl.when((j + s < n_lat) & (j - 1 >= 0))
        def _():
            down.start()

    def grad_z_wait(s):
        up, down = grad_z_copies(s)

        @pl.when((j - s >= 0) & (j + 1 < n_lat))
        def _():
            up.wait_send()

        @pl.when((j + s < n_lat) & (j - 1 >= 0))
        def _():
            down.wait_send()

        @pl.when(j - 1 - s >= 0)
        def _():
            pltpu.make_async_remote_copy(
                src_ref=grad_z.at[0], dst_ref=grad_z.at[lax.max(j - 1 - s, 0)],
                send_sem=gz_send.at[0, s], recv_sem=gz_recv.at[0, s],
                device_id={"lon": i, "lat": lax.max(j - 1, 0)}, device_id_type=MESH,
            ).wait_recv()

        @pl.when(j + 1 + s < n_lat)
        def _():
            pltpu.make_async_remote_copy(
                src_ref=grad_z.at[0], dst_ref=grad_z.at[lax.min(j + 1 + s, n_lat - 1)],
                send_sem=gz_send.at[1, s], recv_sem=gz_recv.at[1, s],
                device_id={"lon": i, "lat": lax.min(j + 1, n_lat - 1)}, device_id_type=MESH,
            ).wait_recv()

    def start_members(m):
        def start(k, c):
            i_to = lax.rem(i + lax.rem(k, n_lon), n_lon)
            j_to = lax.rem(j // 2 * 2 + 2 + k // n_lon, n_lat)
            at = ((i_to // 2) * n_lat + j_to) * share + m

            @pl.when((i_to != i) | (j_to != j))
            def _():
                pltpu.make_async_remote_copy(
                    src_ref=members.at[at, lax.rem(i_to, 2)], dst_ref=taken.at[m, i, lat_rows(j), :],
                    send_sem=m_send.at[m], recv_sem=m_recv.at[m],
                    device_id={"lon": i_to, "lat": j_to}, device_id_type=MESH,
                ).start()

            return c

        lax.fori_loop(0, n, start, 0)

    sent = members.at[pl.ds(0, n - 1), 0]

    def wait_members(m):
        pltpu.make_async_copy(taken.at[m], taken.at[m], m_recv.at[m]).wait()
        pltpu.make_async_copy(sent, sent, m_send.at[m]).wait()

    def grad_all_copy(k):
        i_to = lax.rem(i + k, n_lon)
        return pltpu.make_async_remote_copy(
            src_ref=grad_z.at[:, lax.rem(i_to, 2)], dst_ref=grad_all.at[i],
            send_sem=ga_send.at[i_to], recv_sem=ga_recv.at[i],
            device_id={"lon": i_to, "lat": j}, device_id_type=MESH,
        )

    grad_z_start(0)
    started = 0
    for s in range(n_lat - 1):
        if started < share:
            start_members(started)
            started += 1
        grad_z_wait(s)
        if s + 1 < n_lat - 1:
            grad_z_start(s + 1)
    for k in range(1, n_lon):
        grad_all_copy(k).start()
    for m in range(started, share):
        start_members(m)
    grad_all[i] = grad_z[:, level]
    for k in range(1, n_lon):
        i_from = lax.rem(i + k, n_lon)
        pltpu.make_async_remote_copy(
            src_ref=grad_z.at[:, 0], dst_ref=grad_all.at[i_from],
            send_sem=ga_send.at[i_from], recv_sem=ga_recv.at[i_from],
            device_id={"lon": i_from, "lat": j}, device_id_type=MESH,
        ).wait()

    def pair_term(m, o, along_lon):
        along_lat = jnp.dot(lat_table[...], along_lon, preferred_element_type=jnp.float32)
        x = jnp.concatenate([taken[m, 2 * o], taken[m, 2 * o + 1]], axis=1)
        return x.astype(jnp.float32) * along_lat

    def part_copy(i_to, j_to):
        return pltpu.make_async_remote_copy(
            src_ref=partial.at[i_to, lat_rows(j_to), :], dst_ref=parts.at[level, place],
            send_sem=r_send, recv_sem=r_recv,
            device_id={"lon": i_to, "lat": j_to}, device_id_type=MESH,
        )

    for m in range(share):
        wait_members(m)
        for b in range(n_lon):
            g = grad_all[b].reshape(lat_cells, clon)
            p = (taken[m, b].astype(jnp.float32) * g).astype(jnp.bfloat16)
            for step in (-1, 0, 1):
                o = (b // 2 + step) % pairs
                at = (b % 2 + 2 - 2 * step) * clon
                stack[o * lat_cells:(o + 1) * lat_cells, at:at + clon] = p
        along_lon = jnp.dot(
            stack[...], lon_table[...], preferred_element_type=jnp.float32
        ).astype(jnp.bfloat16)
        if m < share - 1:
            for o in range(pairs):
                term = pair_term(m, o, along_lon[o * lat_cells:(o + 1) * lat_cells])
                total[o] = term if m == 0 else total[o] + term
            continue
        along[...] = along_lon
        for t in range(pairs):
            o = lax.rem(i // 2 + 1 + t, pairs)
            window = along[pl.ds(pl.multiple_of(o * lat_cells, lat_cells), lat_cells), :]
            done = pair_term(m, o, window)
            if share > 1:
                done += total[o]
            for c in range(2):
                partial[2 * o + c] = done[:, c * clon:(c + 1) * clon].astype(jnp.bfloat16)
            for k in range(n_lat):
                j_to = lax.rem(j // 2 * 2 + 2 + k, n_lat)
                for c in range(2):
                    if t < pairs - 1:
                        part_copy(2 * o + c, j_to).start()
                    else:
                        @pl.when((c != level) | (j_to != j))
                        def _():
                            part_copy(2 * o + c, j_to).start()

    kept = pltpu.make_async_copy(partial.at[i, lat_rows(j), :], parts.at[level, place], r_recv)
    kept.start()
    pltpu.make_async_copy(parts, parts, r_recv).wait()
    for l in range(2):
        out[l] = jnp.sum(parts[l].astype(jnp.float32), axis=0) / (count - 1)
    pltpu.make_async_copy(sent, sent, r_send).wait()


def member_plan(members, gradient, lon_taper, lat_taper):
    n_lon, n_lat = lax.axis_size("lon"), lax.axis_size("lat")
    count, levels, clat, clon = members.shape
    share = count // (n_lon // 2 * n_lat)
    lat_cells = n_lat * clat
    n = n_lon * n_lat
    vmem = pl.BlockSpec(memory_space=pltpu.VMEM)
    hbm = pl.BlockSpec(memory_space=pl.ANY)
    dma = pltpu.SemaphoreType.DMA
    return pl.pallas_call(
        functools.partial(member_kernel, n_lon, n_lat, count),
        out_shape=pltpu.VMEM(gradient.shape, jnp.float32),
        in_specs=[hbm, hbm, hbm, hbm],
        out_specs=vmem,
        scratch_shapes=[
            pltpu.VMEM(lon_taper.shape, lon_taper.dtype),
            pltpu.VMEM(lat_taper.shape, lat_taper.dtype),
            pltpu.VMEM((n_lat, levels, clat, clon), jnp.float32),
            pltpu.VMEM((n_lon, n_lat, clat, clon), jnp.float32),
            pltpu.VMEM((share, n_lon, lat_cells, clon), jnp.bfloat16),
            pltpu.VMEM((n_lon // 2 * lat_cells, 6 * clon), jnp.bfloat16),
            pltpu.VMEM((n_lon // 2 * lat_cells, 2 * clon), jnp.bfloat16),
            pltpu.VMEM((n_lon // 2, lat_cells, 2 * clon), jnp.float32),
            pltpu.VMEM((6 * clon, 2 * clon), jnp.bfloat16),
            pltpu.VMEM((lat_cells, lat_cells), jnp.bfloat16),
            pltpu.VMEM((n_lon, lat_cells, clon), jnp.bfloat16),
            pltpu.VMEM((2, n // 2, clat, clon), jnp.bfloat16),
            dma((2,)), dma((2, n_lat)), dma((2, n_lat)), dma, dma((n_lon,)), dma((n_lon,)),
            dma((share,)), dma((share,)), dma, dma,
        ],
        compiler_params=pltpu.CompilerParams(
            collective_id=0, has_side_effects=True, vmem_limit_bytes=VMEM_BYTES
        ),
    )(members, gradient, lon_taper, lat_taper)


def per_device(members, gradient, lon_taper, lat_taper):
    n_lon, n_lat = lax.axis_size("lon"), lax.axis_size("lat")
    count, levels, clat, clon = members.shape
    even = levels == 2 and n_lon % 2 == 0 and n_lon >= 6
    if even and count % (n_lon // 2 * n_lat) == 0 and n_lat * clat % 128 == 0 and n_lat >= 3 and count >= n_lon * n_lat:
        return member_plan(members, gradient, lon_taper, lat_taper)
    return halo_plan(members, gradient, lon_taper, lat_taper)


def solution(mesh):
    in_specs = (P(None, None, "lat", "lon"), P(None, "lat", "lon"), P(), P())
    out_specs = P(None, "lat", "lon")
    return jax.shard_map(
        per_device, mesh=mesh, in_specs=in_specs, out_specs=out_specs, check_vma=False
    )
```

```python
import functools

import jax
import jax.numpy as jnp
from jax import lax
from jax.experimental import pallas as pl
from jax.experimental.pallas import tpu as pltpu
from jax.sharding import PartitionSpec as P

MESH = pl.DeviceIdType.MESH
VMEM_BYTES = 60 * 1024 * 1024
CHUNK = 2


def from_behind(value, axis, steps):
    count = lax.axis_size(axis)
    pairs = [(source, (source + steps) % count) for source in range(count)]
    return lax.ppermute(value, axis, pairs)


def from_behind_2(block, axis, distance):
    devices = range(lax.axis_size(axis))
    route = [(i - distance, i) for i in devices if i - distance in devices]
    return lax.ppermute(block, axis, route)


def taper_table(weights, block_cells):
    half = 2 * block_cells
    rows_at = jnp.arange(5 * block_cells, dtype=jnp.int32)[:, None]
    cols_at = jnp.arange(block_cells, dtype=jnp.int32)[None, :]
    dist = cols_at + half - rows_at
    where_at = jnp.clip(dist + half, 0, 2 * half)
    picked = jnp.take(weights, where_at, axis=0)
    return jnp.where(jnp.abs(dist) <= half, picked, jnp.zeros_like(picked))


def cycle_blocks(values):
    pieces = {}
    for offset in (2, 1, -1, -2):
        pieces[offset] = from_behind(values, "lon", offset)
    return jnp.concatenate([pieces[2], pieces[1], values, pieces[-1], pieces[-2]], axis=3)


def line_blocks(values):
    pieces = {}
    for offset in (2, 1, -1, -2):
        pieces[offset] = from_behind_2(values, "lat", offset)
    return jnp.concatenate([pieces[2], pieces[1], values, pieces[-1], pieces[-2]], axis=2)


def halo_plan(members, gradient, lon_taper, lat_taper):
    clat = gradient.shape[1]
    clon = gradient.shape[2]
    count = members.shape[0]
    products = (members.astype(jnp.float32) * gradient).astype(jnp.bfloat16)
    lon_table = taper_table(lon_taper, clon)
    extended = cycle_blocks(products)
    along_lon = jnp.einsum(
        "mlae,ei->mlai", extended, lon_table, preferred_element_type=jnp.float32
    ).astype(jnp.bfloat16)
    lat_table = taper_table(lat_taper, clat)
    rimmed = line_blocks(along_lon)
    along_lat = jnp.einsum("mlec,ea->mlac", rimmed, lat_table, preferred_element_type=jnp.float32)
    weighted = jnp.sum(members.astype(jnp.float32) * along_lat, axis=0)
    return weighted / (count - 1)


def member_kernel(
    n_lon, n_lat, count,
    members, gradient, lon_taper, lat_taper, out,
    lon_line, lat_line, grad_z, grad_all, taken, stack, along, total, lon_table, lat_table, partial, parts,
    line_sem, gz_send, gz_recv, own_grad, ga_send, ga_recv, m_send, m_recv, r_send, r_recv,
):
    i, j = lax.axis_index("lon"), lax.axis_index("lat")
    clat, clon = gradient.shape[1], gradient.shape[2]
    n = n_lon * n_lat
    share = taken.shape[0]
    half = j // 2
    beside = 2 - half
    mate = 4 * half + 1 - j
    outer = (j == 0) | (j == n_lat - 1)
    frame = taken.shape[2]
    pairs = n_lon // 2
    level = lax.rem(i, 2)
    place = (i // 2) * 2 + lax.rem(j, 2)

    def other(k):
        i_to = lax.rem(i + k // n_lat, n_lon)
        j_to = lax.rem(j + lax.rem(k, n_lat), n_lat)
        return i_to, j_to

    def frame_rows(j_at, in_half):
        return pl.ds(pl.multiple_of((j_at - in_half) * clat, clat), clat)

    lon_in = pltpu.make_async_copy(lon_taper, lon_line, line_sem.at[0])
    lat_in = pltpu.make_async_copy(lat_taper, lat_line, line_sem.at[1])
    lon_in.start()
    lat_in.start()

    barrier = pltpu.get_barrier_semaphore()

    def greet(k, c):
        i_to, j_to = other(k)
        pl.semaphore_signal(barrier, inc=1, device_id={"lon": i_to, "lat": j_to}, device_id_type=MESH)
        return c

    lax.fori_loop(1, n, greet, 0)

    own = pltpu.make_async_copy(gradient, grad_z.at[j - half], own_grad)
    own.start()
    for q in range(share // CHUNK):
        pltpu.make_async_copy(
            members.at[pl.ds(place * share + q * CHUNK, CHUNK), level],
            taken.at[pl.ds(q * CHUNK, CHUNK), i, frame_rows(j, half), :], m_recv.at[q],
        ).start()

    def centred(values, length):
        values = values.astype(jnp.float32).reshape(1, values.shape[0])
        side = (length - values.shape[1] + 1) // 2
        return jnp.pad(values, ((0, 0), (side, side - 1)))

    lon_in.wait()
    lat_in.wait()
    rows, cols = lon_table.shape
    line = 8 * clon
    spread = jnp.broadcast_to(centred(lon_line[...], line), (rows, line))
    turned = pltpu.roll(spread, line - 6 * clon, 1, stride=1, stride_axis=0)
    lon_table[...] = turned[:, :cols].astype(jnp.bfloat16)
    lat_line_cells = 8 * clat
    spread = jnp.broadcast_to(centred(lat_line[...], lat_line_cells), (4 * clat, lat_line_cells))
    turned = pltpu.roll(spread, 4 * clat, 1, stride=1, stride_axis=0)
    whole = turned[:, :4 * clat].T[:frame, :frame]
    to_block = lax.broadcasted_iota(jnp.int32, (frame, frame), 0) // clat
    from_block = lax.broadcasted_iota(jnp.int32, (frame, frame), 1) // clat
    kept_here = (to_block != 2 - 2 * half) | (from_block == 2 * half)
    lat_table[...] = jnp.where(kept_here, whole, 0.0).astype(jnp.bfloat16)

    pl.semaphore_wait(barrier, n - 1)
    own.wait()

    def grad_z_copy(j_to, slot):
        return pltpu.make_async_remote_copy(
            src_ref=gradient, dst_ref=grad_z.at[j - j_to // 2],
            send_sem=gz_send.at[slot], recv_sem=gz_recv.at[j - j_to // 2],
            device_id={"lon": i, "lat": j_to}, device_id_type=MESH,
        )

    across = 2 - 2 * half

    def start_members(q):
        def to_half(first):
            def start(k, c):
                i_to = lax.rem(i + lax.rem(k, n_lon), n_lon)
                j_to = first + lax.rem(j + k // n_lon, 2)
                at = ((i_to // 2) * 2 + lax.rem(j_to, 2)) * share + q * CHUNK

                @pl.when((i_to != i) | (j_to != j))
                def _():
                    pltpu.make_async_remote_copy(
                        src_ref=members.at[pl.ds(at, CHUNK), lax.rem(i_to, 2)],
                        dst_ref=taken.at[pl.ds(q * CHUNK, CHUNK), i, frame_rows(j, first // 2), :],
                        send_sem=m_send.at[q], recv_sem=m_recv.at[q],
                        device_id={"lon": i_to, "lat": j_to}, device_id_type=MESH,
                    ).start()

                return c

            lax.fori_loop(0, 2 * n_lon, start, 0)

        @pl.when(jnp.logical_not(outer))
        def _():
            to_half(across)

        to_half(2 * half)

    def wait_blocks(count, sem):
        sent = members.at[pl.ds(0, count), 0]
        pltpu.make_async_copy(sent, sent, sem).wait()

    def wait_members(q):
        here = taken.at[pl.ds(q * CHUNK, CHUNK)]
        pltpu.make_async_copy(here, here, m_recv.at[q]).wait()
        wait_blocks((n // 2 - 1) * CHUNK, m_send.at[q])

        @pl.when(jnp.logical_not(outer))
        def _():
            wait_blocks(n // 2 * CHUNK, m_send.at[q])

    def grad_all_copy(k):
        i_to = lax.rem(i + k, n_lon)
        return pltpu.make_async_remote_copy(
            src_ref=grad_z.at[:, lax.rem(i_to, 2)], dst_ref=grad_all.at[i],
            send_sem=ga_send.at[i_to], recv_sem=ga_recv.at[i],
            device_id={"lon": i_to, "lat": j}, device_id_type=MESH,
        )

    @pl.when(jnp.logical_not(outer))
    def _():
        for c in range(2):
            grad_z_copy(across + c, 1 + c).start()

    grad_z_copy(mate, 0).start()
    start_members(0)
    grad_z_copy(mate, 0).wait_send()

    @pl.when(jnp.logical_not(outer))
    def _():
        for c in range(2):
            grad_z_copy(across + c, 1 + c).wait_send()

    for j_from in (mate, beside):
        pltpu.make_async_remote_copy(
            src_ref=gradient, dst_ref=grad_z.at[j_from - half],
            send_sem=gz_send.at[0], recv_sem=gz_recv.at[j_from - half],
            device_id={"lon": i, "lat": j_from}, device_id_type=MESH,
        ).wait_recv()
    for k in range(1, n_lon):
        grad_all_copy(k).start()
    for q in range(1, share // CHUNK):
        start_members(q)
    grad_all[i] = grad_z[:, level]
    for k in range(1, n_lon):
        i_from = lax.rem(i + k, n_lon)
        pltpu.make_async_remote_copy(
            src_ref=grad_z.at[:, 0], dst_ref=grad_all.at[i_from],
            send_sem=ga_send.at[i_from], recv_sem=ga_recv.at[i_from],
            device_id={"lon": i_from, "lat": j}, device_id_type=MESH,
        ).wait()

    def pair_term(m, o, along_lon):
        along_lat = jnp.dot(lat_table[...], along_lon, preferred_element_type=jnp.float32)
        x = jnp.concatenate([taken[m, 2 * o], taken[m, 2 * o + 1]], axis=1)
        return x.astype(jnp.float32) * along_lat

    def part_copy(i_to, j_to, crosses):
        return pltpu.make_async_remote_copy(
            src_ref=partial.at[i_to, frame_rows(j_to, half), :], dst_ref=parts.at[crosses, level, place],
            send_sem=r_send, recv_sem=r_recv,
            device_id={"lon": i_to, "lat": j_to}, device_id_type=MESH,
        )

    span = CHUNK * frame
    for q in range(share // CHUNK):
        wait_members(q)
        for b in range(n_lon):
            g = grad_all[b].reshape(frame, clon)
            for e in range(CHUNK):
                p = (taken[q * CHUNK + e, b].astype(jnp.float32) * g).astype(jnp.bfloat16)
                for step in (-1, 0, 1):
                    o = (b // 2 + step) % pairs
                    at = (b % 2 + 2 - 2 * step) * clon
                    row = o * span + e * frame
                    stack[row:row + frame, at:at + clon] = p
        along_lon = jnp.dot(
            stack[...], lon_table[...], preferred_element_type=jnp.float32
        ).astype(jnp.bfloat16)
        if q < share // CHUNK - 1:
            for o in range(pairs):
                for e in range(CHUNK):
                    row = o * span + e * frame
                    term = pair_term(q * CHUNK + e, o, along_lon[row:row + frame])
                    total[o] = term if q + e == 0 else total[o] + term
            continue
        along[...] = along_lon
        for t in range(pairs):
            o = lax.rem(i // 2 + 1 + t, pairs)
            done = total[o]
            for e in range(CHUNK):
                row = pl.multiple_of(o * span + e * frame, clat)
                done += pair_term(q * CHUNK + e, o, along[pl.ds(row, frame), :])
            for c in range(2):
                partial[2 * o + c] = done[:, c * clon:(c + 1) * clon].astype(jnp.bfloat16)
            for c in range(2):
                part_copy(2 * o + c, beside, 1).start()
            for c in range(2):
                part_copy(2 * o + c, mate, 0).start()
            for c in range(2):
                if t < pairs - 1:
                    part_copy(2 * o + c, j, 0).start()
                else:
                    @pl.when(c != level)
                    def _():
                        part_copy(2 * o + c, j, 0).start()

    kept = pltpu.make_async_copy(
        partial.at[i, frame_rows(j, half), :], parts.at[0, level, place], r_recv
    )
    kept.start()

    def add_up(sets):
        for l in range(2):
            sums = [jnp.sum(parts[s, l].astype(jnp.float32), axis=0) for s in range(sets)]
            out[l] = sum(sums) / (count - 1)

    @pl.when(outer)
    def _():
        pltpu.make_async_copy(parts.at[0], parts.at[0], r_recv).wait()
        add_up(1)

    @pl.when(jnp.logical_not(outer))
    def _():
        pltpu.make_async_copy(parts, parts, r_recv).wait()
        add_up(2)

    wait_blocks(3 * n_lon - 1, r_send)


def member_plan(members, gradient, lon_taper, lat_taper):
    n_lon, n_lat = lax.axis_size("lon"), lax.axis_size("lat")
    count, levels, clat, clon = members.shape
    share = count // n_lon
    frame = 3 * clat
    vmem = pl.BlockSpec(memory_space=pltpu.VMEM)
    hbm = pl.BlockSpec(memory_space=pl.ANY)
    dma = pltpu.SemaphoreType.DMA
    return pl.pallas_call(
        functools.partial(member_kernel, n_lon, n_lat, count),
        out_shape=pltpu.VMEM(gradient.shape, jnp.float32),
        in_specs=[hbm, hbm, hbm, hbm],
        out_specs=vmem,
        scratch_shapes=[
            pltpu.VMEM(lon_taper.shape, lon_taper.dtype),
            pltpu.VMEM(lat_taper.shape, lat_taper.dtype),
            pltpu.VMEM((3, levels, clat, clon), jnp.float32),
            pltpu.VMEM((n_lon, 3, clat, clon), jnp.float32),
            pltpu.VMEM((share, n_lon, frame, clon), jnp.bfloat16),
            pltpu.VMEM((n_lon // 2 * CHUNK * frame, 6 * clon), jnp.bfloat16),
            pltpu.VMEM((n_lon // 2 * CHUNK * frame, 2 * clon), jnp.bfloat16),
            pltpu.VMEM((n_lon // 2, frame, 2 * clon), jnp.float32),
            pltpu.VMEM((6 * clon, 2 * clon), jnp.bfloat16),
            pltpu.VMEM((frame, frame), jnp.bfloat16),
            pltpu.VMEM((n_lon, frame, clon), jnp.bfloat16),
            pltpu.VMEM((2, 2, n_lon, clat, clon), jnp.bfloat16),
            dma((2,)), dma((3,)), dma((3,)), dma, dma((n_lon,)), dma((n_lon,)),
            dma((share // CHUNK,)), dma((share // CHUNK,)), dma, dma,
        ],
        compiler_params=pltpu.CompilerParams(
            collective_id=0, has_side_effects=True, vmem_limit_bytes=VMEM_BYTES
        ),
    )(members, gradient, lon_taper, lat_taper)


def per_device(members, gradient, lon_taper, lat_taper):
    n_lon, n_lat = lax.axis_size("lon"), lax.axis_size("lat")
    count, levels, clat, clon = members.shape
    cycle = levels == 2 and n_lon % 2 == 0 and n_lon >= 6
    if cycle and n_lat == 4 and count % (n_lon * CHUNK) == 0 and count >= n_lon * n_lat * CHUNK:
        return member_plan(members, gradient, lon_taper, lat_taper)
    return halo_plan(members, gradient, lon_taper, lat_taper)


def solution(mesh):
    in_specs = (P(None, None, "lat", "lon"), P(None, "lat", "lon"), P(), P())
    out_specs = P(None, "lat", "lon")
    return jax.shard_map(
        per_device, mesh=mesh, in_specs=in_specs, out_specs=out_specs, check_vma=False
    )
```

```python
import functools

import jax
import jax.numpy as jnp
from jax import lax
from jax.experimental import pallas as pl
from jax.experimental.pallas import tpu as pltpu
from jax.sharding import PartitionSpec as P

MESH = pl.DeviceIdType.MESH
VMEM_BYTES = 60 * 1024 * 1024
CHUNK = 2


def from_behind(value, axis, steps):
    count = lax.axis_size(axis)
    pairs = [(source, (source + steps) % count) for source in range(count)]
    return lax.ppermute(value, axis, pairs)


def from_behind_2(block, axis, distance):
    devices = range(lax.axis_size(axis))
    route = [(i - distance, i) for i in devices if i - distance in devices]
    return lax.ppermute(block, axis, route)


def taper_table(weights, block_cells):
    half = 2 * block_cells
    rows_at = jnp.arange(5 * block_cells, dtype=jnp.int32)[:, None]
    cols_at = jnp.arange(block_cells, dtype=jnp.int32)[None, :]
    dist = cols_at + half - rows_at
    where_at = jnp.clip(dist + half, 0, 2 * half)
    picked = jnp.take(weights, where_at, axis=0)
    return jnp.where(jnp.abs(dist) <= half, picked, jnp.zeros_like(picked))


def cycle_blocks(values):
    pieces = {}
    for offset in (2, 1, -1, -2):
        pieces[offset] = from_behind(values, "lon", offset)
    return jnp.concatenate([pieces[2], pieces[1], values, pieces[-1], pieces[-2]], axis=3)


def line_blocks(values):
    pieces = {}
    for offset in (2, 1, -1, -2):
        pieces[offset] = from_behind_2(values, "lat", offset)
    return jnp.concatenate([pieces[2], pieces[1], values, pieces[-1], pieces[-2]], axis=2)


def halo_plan(members, gradient, lon_taper, lat_taper):
    clat = gradient.shape[1]
    clon = gradient.shape[2]
    count = members.shape[0]
    products = (members.astype(jnp.float32) * gradient).astype(jnp.bfloat16)
    lon_table = taper_table(lon_taper, clon)
    extended = cycle_blocks(products)
    along_lon = jnp.einsum(
        "mlae,ei->mlai", extended, lon_table, preferred_element_type=jnp.float32
    ).astype(jnp.bfloat16)
    lat_table = taper_table(lat_taper, clat)
    rimmed = line_blocks(along_lon)
    along_lat = jnp.einsum("mlec,ea->mlac", rimmed, lat_table, preferred_element_type=jnp.float32)
    weighted = jnp.sum(members.astype(jnp.float32) * along_lat, axis=0)
    return weighted / (count - 1)


def member_kernel(
    n_lon, n_lat, count,
    members, gradient, lon_taper, lat_taper, out,
    lon_line, lat_line, grad_z, grad_all, taken, stack, total, lon_table, lat_table, partial, parts,
    line_sem, gz_send, gz_recv, own_grad, ga_send, ga_recv, m_send, m_recv, r_send, r_recv,
):
    i, j = lax.axis_index("lon"), lax.axis_index("lat")
    clat, clon = gradient.shape[1], gradient.shape[2]
    n = n_lon * n_lat
    share = taken.shape[0]
    half = j // 2
    beside = 2 - half
    mate = 4 * half + 1 - j
    outer = (j == 0) | (j == n_lat - 1)
    frame = taken.shape[2]
    pairs = n_lon // 2
    level = lax.rem(i, 2)
    place = (i // 2) * 2 + lax.rem(j, 2)

    def other(k):
        i_to = lax.rem(i + k // n_lat, n_lon)
        j_to = lax.rem(j + lax.rem(k, n_lat), n_lat)
        return i_to, j_to

    def frame_rows(j_at, in_half):
        return pl.ds(pl.multiple_of((j_at - in_half) * clat, clat), clat)

    lon_in = pltpu.make_async_copy(lon_taper, lon_line, line_sem.at[0])
    lat_in = pltpu.make_async_copy(lat_taper, lat_line, line_sem.at[1])
    lon_in.start()
    lat_in.start()

    barrier = pltpu.get_barrier_semaphore()

    def greet(k, c):
        i_to, j_to = other(k)
        pl.semaphore_signal(barrier, inc=1, device_id={"lon": i_to, "lat": j_to}, device_id_type=MESH)
        return c

    lax.fori_loop(1, n, greet, 0)

    own = pltpu.make_async_copy(gradient, grad_z.at[j - half], own_grad)
    own.start()
    for q in range(share // CHUNK):
        pltpu.make_async_copy(
            members.at[pl.ds(place * share + q * CHUNK, CHUNK), level],
            taken.at[pl.ds(q * CHUNK, CHUNK), i, frame_rows(j, half), :], m_recv.at[q],
        ).start()

    def centred(values, length):
        values = values.astype(jnp.float32).reshape(1, values.shape[0])
        side = (length - values.shape[1] + 1) // 2
        return jnp.pad(values, ((0, 0), (side, side - 1)))

    lon_in.wait()
    lat_in.wait()
    rows, cols = lon_table.shape
    line = 8 * clon
    spread = jnp.broadcast_to(centred(lon_line[...], line), (rows, line))
    turned = pltpu.roll(spread, line - 6 * clon, 1, stride=1, stride_axis=0)
    lon_table[...] = turned[:, :cols].astype(jnp.bfloat16)
    lat_line_cells = 8 * clat
    spread = jnp.broadcast_to(centred(lat_line[...], lat_line_cells), (4 * clat, lat_line_cells))
    turned = pltpu.roll(spread, 4 * clat, 1, stride=1, stride_axis=0)
    whole = turned[:, :4 * clat].T[:frame, :frame]
    to_block = lax.broadcasted_iota(jnp.int32, (frame, frame), 0) // clat
    from_block = lax.broadcasted_iota(jnp.int32, (frame, frame), 1) // clat
    kept_here = (to_block != 2 - 2 * half) | (from_block == 2 * half)
    lat_table[...] = jnp.where(kept_here, whole, 0.0).astype(jnp.bfloat16)

    pl.semaphore_wait(barrier, n - 1)
    own.wait()

    def grad_z_copy(j_to, slot):
        return pltpu.make_async_remote_copy(
            src_ref=gradient, dst_ref=grad_z.at[j - j_to // 2],
            send_sem=gz_send.at[slot], recv_sem=gz_recv.at[j - j_to // 2],
            device_id={"lon": i, "lat": j_to}, device_id_type=MESH,
        )

    across = 2 - 2 * half

    def start_members(q):
        def to_half(first):
            def start(k, c):
                i_to = lax.rem(i + lax.rem(k, n_lon), n_lon)
                j_to = first + lax.rem(j + k // n_lon, 2)
                at = ((i_to // 2) * 2 + lax.rem(j_to, 2)) * share + q * CHUNK

                @pl.when((i_to != i) | (j_to != j))
                def _():
                    pltpu.make_async_remote_copy(
                        src_ref=members.at[pl.ds(at, CHUNK), lax.rem(i_to, 2)],
                        dst_ref=taken.at[pl.ds(q * CHUNK, CHUNK), i, frame_rows(j, first // 2), :],
                        send_sem=m_send.at[q], recv_sem=m_recv.at[q],
                        device_id={"lon": i_to, "lat": j_to}, device_id_type=MESH,
                    ).start()

                return c

            lax.fori_loop(0, 2 * n_lon, start, 0)

        @pl.when(jnp.logical_not(outer))
        def _():
            to_half(across)

        to_half(2 * half)

    def wait_blocks(count, sem):
        sent = members.at[pl.ds(0, count), 0]
        pltpu.make_async_copy(sent, sent, sem).wait()

    def wait_members(q):
        here = taken.at[pl.ds(q * CHUNK, CHUNK)]
        pltpu.make_async_copy(here, here, m_recv.at[q]).wait()
        wait_blocks((n // 2 - 1) * CHUNK, m_send.at[q])

        @pl.when(jnp.logical_not(outer))
        def _():
            wait_blocks(n // 2 * CHUNK, m_send.at[q])

    def grad_all_copy(k):
        i_to = lax.rem(i + k, n_lon)
        return pltpu.make_async_remote_copy(
            src_ref=grad_z.at[:, lax.rem(i_to, 2)], dst_ref=grad_all.at[i],
            send_sem=ga_send.at[i_to], recv_sem=ga_recv.at[i],
            device_id={"lon": i_to, "lat": j}, device_id_type=MESH,
        )

    @pl.when(jnp.logical_not(outer))
    def _():
        for c in range(2):
            grad_z_copy(across + c, 1 + c).start()

    grad_z_copy(mate, 0).start()
    start_members(0)
    grad_z_copy(mate, 0).wait_send()

    @pl.when(jnp.logical_not(outer))
    def _():
        for c in range(2):
            grad_z_copy(across + c, 1 + c).wait_send()

    for j_from in (mate, beside):
        pltpu.make_async_remote_copy(
            src_ref=gradient, dst_ref=grad_z.at[j_from - half],
            send_sem=gz_send.at[0], recv_sem=gz_recv.at[j_from - half],
            device_id={"lon": i, "lat": j_from}, device_id_type=MESH,
        ).wait_recv()
    for k in range(1, n_lon):
        grad_all_copy(k).start()
    for q in range(1, share // CHUNK):
        start_members(q)
    grad_all[i] = grad_z[:, level]
    for k in range(1, n_lon):
        i_from = lax.rem(i + k, n_lon)
        pltpu.make_async_remote_copy(
            src_ref=grad_z.at[:, 0], dst_ref=grad_all.at[i_from],
            send_sem=ga_send.at[i_from], recv_sem=ga_recv.at[i_from],
            device_id={"lon": i_from, "lat": j}, device_id_type=MESH,
        ).wait()

    def pair_term(m, o, along_lon):
        along_lat = jnp.dot(lat_table[...], along_lon, preferred_element_type=jnp.float32)
        x = jnp.concatenate([taken[m, 2 * o], taken[m, 2 * o + 1]], axis=1)
        return x.astype(jnp.float32) * along_lat

    def part_copy(i_to, j_to, crosses):
        return pltpu.make_async_remote_copy(
            src_ref=partial.at[i_to, frame_rows(j_to, half), :], dst_ref=parts.at[crosses, level, place],
            send_sem=r_send, recv_sem=r_recv,
            device_id={"lon": i_to, "lat": j_to}, device_id_type=MESH,
        )

    span = CHUNK * frame
    for q in range(share // CHUNK):
        wait_members(q)
        for b in range(n_lon):
            g = grad_all[b].reshape(frame, clon)
            for e in range(CHUNK):
                p = (taken[q * CHUNK + e, b].astype(jnp.float32) * g).astype(jnp.bfloat16)
                for step in (-1, 0, 1):
                    o = (b // 2 + step) % pairs
                    at = (b % 2 + 2 - 2 * step) * clon
                    row = o * span + e * frame
                    stack[row:row + frame, at:at + clon] = p
        if q < share // CHUNK - 1:
            along_lon = jnp.dot(
                stack[...], lon_table[...], preferred_element_type=jnp.float32
            ).astype(jnp.bfloat16)
            for o in range(pairs):
                for e in range(CHUNK):
                    row = o * span + e * frame
                    term = pair_term(q * CHUNK + e, o, along_lon[row:row + frame])
                    total[o] = term if q + e == 0 else total[o] + term
            continue
        for t in range(pairs):
            o = lax.rem(i // 2 + 1 + t, pairs)
            window = stack[pl.ds(pl.multiple_of(o * span, span), span), :]
            along_lon = jnp.dot(
                window, lon_table[...], preferred_element_type=jnp.float32
            ).astype(jnp.bfloat16)
            done = total[o]
            for e in range(CHUNK):
                row = e * frame
                done += pair_term(q * CHUNK + e, o, along_lon[row:row + frame])
            for c in range(2):
                partial[2 * o + c] = done[:, c * clon:(c + 1) * clon].astype(jnp.bfloat16)
            for c in range(2):
                part_copy(2 * o + c, beside, 1).start()
            for c in range(2):
                part_copy(2 * o + c, mate, 0).start()
            for c in range(2):
                if t < pairs - 1:
                    part_copy(2 * o + c, j, 0).start()
                else:
                    @pl.when(c != level)
                    def _():
                        part_copy(2 * o + c, j, 0).start()

    kept = pltpu.make_async_copy(
        partial.at[i, frame_rows(j, half), :], parts.at[0, level, place], r_recv
    )
    kept.start()

    def add_up(sets):
        for l in range(2):
            sums = [jnp.sum(parts[s, l].astype(jnp.float32), axis=0) for s in range(sets)]
            out[l] = sum(sums) / (count - 1)

    @pl.when(outer)
    def _():
        pltpu.make_async_copy(parts.at[0], parts.at[0], r_recv).wait()
        add_up(1)

    @pl.when(jnp.logical_not(outer))
    def _():
        pltpu.make_async_copy(parts, parts, r_recv).wait()
        add_up(2)

    wait_blocks(3 * n_lon - 1, r_send)


def member_plan(members, gradient, lon_taper, lat_taper):
    n_lon, n_lat = lax.axis_size("lon"), lax.axis_size("lat")
    count, levels, clat, clon = members.shape
    share = count // n_lon
    frame = 3 * clat
    vmem = pl.BlockSpec(memory_space=pltpu.VMEM)
    hbm = pl.BlockSpec(memory_space=pl.ANY)
    dma = pltpu.SemaphoreType.DMA
    return pl.pallas_call(
        functools.partial(member_kernel, n_lon, n_lat, count),
        out_shape=pltpu.VMEM(gradient.shape, jnp.float32),
        in_specs=[hbm, hbm, hbm, hbm],
        out_specs=vmem,
        scratch_shapes=[
            pltpu.VMEM(lon_taper.shape, lon_taper.dtype),
            pltpu.VMEM(lat_taper.shape, lat_taper.dtype),
            pltpu.VMEM((3, levels, clat, clon), jnp.float32),
            pltpu.VMEM((n_lon, 3, clat, clon), jnp.float32),
            pltpu.VMEM((share, n_lon, frame, clon), jnp.bfloat16),
            pltpu.VMEM((n_lon // 2 * CHUNK * frame, 6 * clon), jnp.bfloat16),
            pltpu.VMEM((n_lon // 2, frame, 2 * clon), jnp.float32),
            pltpu.VMEM((6 * clon, 2 * clon), jnp.bfloat16),
            pltpu.VMEM((frame, frame), jnp.bfloat16),
            pltpu.VMEM((n_lon, frame, clon), jnp.bfloat16),
            pltpu.VMEM((2, 2, n_lon, clat, clon), jnp.bfloat16),
            dma((2,)), dma((3,)), dma((3,)), dma, dma((n_lon,)), dma((n_lon,)),
            dma((share // CHUNK,)), dma((share // CHUNK,)), dma, dma,
        ],
        compiler_params=pltpu.CompilerParams(
            collective_id=0, has_side_effects=True, vmem_limit_bytes=VMEM_BYTES
        ),
    )(members, gradient, lon_taper, lat_taper)


def per_device(members, gradient, lon_taper, lat_taper):
    n_lon, n_lat = lax.axis_size("lon"), lax.axis_size("lat")
    count, levels, clat, clon = members.shape
    cycle = levels == 2 and n_lon % 2 == 0 and n_lon >= 6
    if cycle and n_lat == 4 and count % (n_lon * CHUNK) == 0 and count >= n_lon * n_lat * CHUNK:
        return member_plan(members, gradient, lon_taper, lat_taper)
    return halo_plan(members, gradient, lon_taper, lat_taper)


def solution(mesh):
    in_specs = (P(None, None, "lat", "lon"), P(None, "lat", "lon"), P(), P())
    out_specs = P(None, "lat", "lon")
    return jax.shard_map(
        per_device, mesh=mesh, in_specs=in_specs, out_specs=out_specs, check_vma=False
    )
```

```python
import functools

import jax
import jax.numpy as jnp
from jax import lax
from jax.experimental import pallas as pl
from jax.experimental.pallas import tpu as pltpu
from jax.sharding import PartitionSpec as P

MESH = pl.DeviceIdType.MESH
VMEM_BYTES = 60 * 1024 * 1024
CHUNK = 2


def from_behind(value, axis, steps):
    count = lax.axis_size(axis)
    pairs = [(source, (source + steps) % count) for source in range(count)]
    return lax.ppermute(value, axis, pairs)


def from_behind_2(block, axis, distance):
    devices = range(lax.axis_size(axis))
    route = [(i - distance, i) for i in devices if i - distance in devices]
    return lax.ppermute(block, axis, route)


def taper_table(weights, block_cells):
    half = 2 * block_cells
    rows_at = jnp.arange(5 * block_cells, dtype=jnp.int32)[:, None]
    cols_at = jnp.arange(block_cells, dtype=jnp.int32)[None, :]
    dist = cols_at + half - rows_at
    where_at = jnp.clip(dist + half, 0, 2 * half)
    picked = jnp.take(weights, where_at, axis=0)
    return jnp.where(jnp.abs(dist) <= half, picked, jnp.zeros_like(picked))


def cycle_blocks(values):
    pieces = {}
    for offset in (2, 1, -1, -2):
        pieces[offset] = from_behind(values, "lon", offset)
    return jnp.concatenate([pieces[2], pieces[1], values, pieces[-1], pieces[-2]], axis=3)


def line_blocks(values):
    pieces = {}
    for offset in (2, 1, -1, -2):
        pieces[offset] = from_behind_2(values, "lat", offset)
    return jnp.concatenate([pieces[2], pieces[1], values, pieces[-1], pieces[-2]], axis=2)


def halo_plan(members, gradient, lon_taper, lat_taper):
    clat = gradient.shape[1]
    clon = gradient.shape[2]
    count = members.shape[0]
    products = (members.astype(jnp.float32) * gradient).astype(jnp.bfloat16)
    lon_table = taper_table(lon_taper, clon)
    extended = cycle_blocks(products)
    along_lon = jnp.einsum(
        "mlae,ei->mlai", extended, lon_table, preferred_element_type=jnp.float32
    ).astype(jnp.bfloat16)
    lat_table = taper_table(lat_taper, clat)
    rimmed = line_blocks(along_lon)
    along_lat = jnp.einsum("mlec,ea->mlac", rimmed, lat_table, preferred_element_type=jnp.float32)
    weighted = jnp.sum(members.astype(jnp.float32) * along_lat, axis=0)
    return weighted / (count - 1)


def member_kernel(
    n_lon, n_lat, count,
    members, gradient, lon_taper, lat_taper, out,
    lon_line, lat_line, grad_z, grad_all, taken, stack, along, total, lon_table, lat_table, partial, parts,
    line_sem, gz_send, gz_recv, own_grad, ga_send, ga_recv, m_send, m_recv, r_send, r_recv,
):
    i, j = lax.axis_index("lon"), lax.axis_index("lat")
    clat, clon = gradient.shape[1], gradient.shape[2]
    n = n_lon * n_lat
    share = taken.shape[0]
    half = j // 2
    beside = 2 - half
    mate = 4 * half + 1 - j
    outer = (j == 0) | (j == n_lat - 1)
    frame = taken.shape[2]
    pairs = n_lon // 2
    level = lax.rem(i, 2)
    place = (i // 2) * 2 + lax.rem(j, 2)

    def other(k):
        i_to = lax.rem(i + k // n_lat, n_lon)
        j_to = lax.rem(j + lax.rem(k, n_lat), n_lat)
        return i_to, j_to

    def frame_rows(j_at, in_half):
        return pl.ds(pl.multiple_of((j_at - in_half) * clat, clat), clat)

    barrier = pltpu.get_barrier_semaphore()

    def greet(k, c):
        i_to, j_to = other(k)

        @pl.when((j_to - j != n_lat - 1) & (j - j_to != n_lat - 1))
        def _():
            pl.semaphore_signal(barrier, inc=1, device_id={"lon": i_to, "lat": j_to}, device_id_type=MESH)

        return c

    lax.fori_loop(1, n, greet, 0)

    @pl.when(outer)
    def _():
        pl.semaphore_wait(barrier, n - n_lon - 1)

    @pl.when(jnp.logical_not(outer))
    def _():
        pl.semaphore_wait(barrier, n - 1)


    def grad_z_copy(j_to, slot):
        return pltpu.make_async_remote_copy(
            src_ref=gradient, dst_ref=grad_z.at[j - j_to // 2],
            send_sem=gz_send.at[slot], recv_sem=gz_recv.at[j - j_to // 2],
            device_id={"lon": i, "lat": j_to}, device_id_type=MESH,
        )

    across = 2 - 2 * half

    def start_members(q):
        def to_half(first):
            def start(k, c):
                i_to = lax.rem(i + lax.rem(k, n_lon), n_lon)
                j_to = first + lax.rem(j + k // n_lon, 2)
                at = ((i_to // 2) * 2 + lax.rem(j_to, 2)) * share + q * CHUNK

                @pl.when((i_to != i) | (j_to != j))
                def _():
                    pltpu.make_async_remote_copy(
                        src_ref=members.at[pl.ds(at, CHUNK), lax.rem(i_to, 2)],
                        dst_ref=taken.at[pl.ds(q * CHUNK, CHUNK), i, frame_rows(j, first // 2), :],
                        send_sem=m_send.at[q], recv_sem=m_recv.at[q],
                        device_id={"lon": i_to, "lat": j_to}, device_id_type=MESH,
                    ).start()

                return c

            lax.fori_loop(0, 2 * n_lon, start, 0)

        @pl.when(jnp.logical_not(outer))
        def _():
            to_half(across)

        to_half(2 * half)

    def wait_blocks(count, sem):
        sent = members.at[pl.ds(0, count), 0]
        pltpu.make_async_copy(sent, sent, sem).wait()

    def wait_members(q):
        here = taken.at[pl.ds(q * CHUNK, CHUNK)]
        pltpu.make_async_copy(here, here, m_recv.at[q]).wait()
        wait_blocks((n // 2 - 1) * CHUNK, m_send.at[q])

        @pl.when(jnp.logical_not(outer))
        def _():
            wait_blocks(n // 2 * CHUNK, m_send.at[q])

    def grad_all_copy(k):
        i_to = lax.rem(i + k, n_lon)
        return pltpu.make_async_remote_copy(
            src_ref=grad_z.at[:, lax.rem(i_to, 2)], dst_ref=grad_all.at[i],
            send_sem=ga_send.at[i_to], recv_sem=ga_recv.at[i],
            device_id={"lon": i_to, "lat": j}, device_id_type=MESH,
        )

    @pl.when(jnp.logical_not(outer))
    def _():
        for c in range(2):
            grad_z_copy(across + c, 1 + c).start()

    grad_z_copy(mate, 0).start()
    start_members(0)
    lon_in = pltpu.make_async_copy(lon_taper, lon_line, line_sem.at[0])
    lat_in = pltpu.make_async_copy(lat_taper, lat_line, line_sem.at[1])
    lon_in.start()
    lat_in.start()

    own = pltpu.make_async_copy(gradient, grad_z.at[j - half], own_grad)
    own.start()
    for q in range(share // CHUNK):
        pltpu.make_async_copy(
            members.at[pl.ds(place * share + q * CHUNK, CHUNK), level],
            taken.at[pl.ds(q * CHUNK, CHUNK), i, frame_rows(j, half), :], m_recv.at[q],
        ).start()

    own.wait()
    grad_z_copy(mate, 0).wait_send()

    @pl.when(jnp.logical_not(outer))
    def _():
        for c in range(2):
            grad_z_copy(across + c, 1 + c).wait_send()

    for j_from in (mate, beside):
        pltpu.make_async_remote_copy(
            src_ref=gradient, dst_ref=grad_z.at[j_from - half],
            send_sem=gz_send.at[0], recv_sem=gz_recv.at[j_from - half],
            device_id={"lon": i, "lat": j_from}, device_id_type=MESH,
        ).wait_recv()
    for k in range(1, n_lon):
        grad_all_copy(k).start()
    for q in range(1, share // CHUNK):
        start_members(q)
    def centred(values, length):
        values = values.astype(jnp.float32).reshape(1, values.shape[0])
        side = (length - values.shape[1] + 1) // 2
        return jnp.pad(values, ((0, 0), (side, side - 1)))

    lon_in.wait()
    lat_in.wait()
    rows, cols = lon_table.shape
    line = 8 * clon
    spread = jnp.broadcast_to(centred(lon_line[...], line), (rows, line))
    turned = pltpu.roll(spread, line - 6 * clon, 1, stride=1, stride_axis=0)
    lon_table[...] = turned[:, :cols].astype(jnp.bfloat16)
    lat_line_cells = 8 * clat
    spread = jnp.broadcast_to(centred(lat_line[...], lat_line_cells), (4 * clat, lat_line_cells))
    turned = pltpu.roll(spread, 4 * clat, 1, stride=1, stride_axis=0)
    whole = turned[:, :4 * clat].T[:frame, :frame]
    to_block = lax.broadcasted_iota(jnp.int32, (frame, frame), 0) // clat
    from_block = lax.broadcasted_iota(jnp.int32, (frame, frame), 1) // clat
    kept_here = (to_block != 2 - 2 * half) | (from_block == 2 * half)
    lat_table[...] = jnp.where(kept_here, whole, 0.0).astype(jnp.bfloat16)

    grad_all[i] = grad_z[:, level]
    for k in range(1, n_lon):
        i_from = lax.rem(i + k, n_lon)
        pltpu.make_async_remote_copy(
            src_ref=grad_z.at[:, 0], dst_ref=grad_all.at[i_from],
            send_sem=ga_send.at[i_from], recv_sem=ga_recv.at[i_from],
            device_id={"lon": i_from, "lat": j}, device_id_type=MESH,
        ).wait()

    def pair_term(m, o, along_lon):
        along_lat = jnp.dot(lat_table[...], along_lon, preferred_element_type=jnp.float32)
        x = jnp.concatenate([taken[m, 2 * o], taken[m, 2 * o + 1]], axis=1)
        return x.astype(jnp.float32) * along_lat

    def part_copy(i_to, j_to, crosses):
        return pltpu.make_async_remote_copy(
            src_ref=partial.at[i_to, frame_rows(j_to, half), :], dst_ref=parts.at[crosses, level, place],
            send_sem=r_send, recv_sem=r_recv,
            device_id={"lon": i_to, "lat": j_to}, device_id_type=MESH,
        )

    span = CHUNK * frame
    for q in range(share // CHUNK):
        wait_members(q)
        for b in range(n_lon):
            g = grad_all[b].reshape(frame, clon)
            for e in range(CHUNK):
                p = (taken[q * CHUNK + e, b].astype(jnp.float32) * g).astype(jnp.bfloat16)
                for step in (-1, 0, 1):
                    o = (b // 2 + step) % pairs
                    at = (b % 2 + 2 - 2 * step) * clon
                    row = o * span + e * frame
                    stack[row:row + frame, at:at + clon] = p
        along_lon = jnp.dot(
            stack[...], lon_table[...], preferred_element_type=jnp.float32
        ).astype(jnp.bfloat16)
        if q < share // CHUNK - 1:
            for o in range(pairs):
                for e in range(CHUNK):
                    row = o * span + e * frame
                    term = pair_term(q * CHUNK + e, o, along_lon[row:row + frame])
                    total[o] = term if q + e == 0 else total[o] + term
            continue
        along[...] = along_lon
        for t in range(pairs):
            o = lax.rem(i // 2 + 1 + t, pairs)
            done = total[o]
            for e in range(CHUNK):
                row = pl.multiple_of(o * span + e * frame, clat)
                done += pair_term(q * CHUNK + e, o, along[pl.ds(row, frame), :])
            for c in range(2):
                partial[2 * o + c] = done[:, c * clon:(c + 1) * clon].astype(jnp.bfloat16)
            for c in range(2):
                part_copy(2 * o + c, beside, 1).start()
            for c in range(2):
                part_copy(2 * o + c, mate, 0).start()
            for c in range(2):
                if t < pairs - 1:
                    part_copy(2 * o + c, j, 0).start()
                else:
                    @pl.when(c != level)
                    def _():
                        part_copy(2 * o + c, j, 0).start()

    kept = pltpu.make_async_copy(
        partial.at[i, frame_rows(j, half), :], parts.at[0, level, place], r_recv
    )
    kept.start()

    def add_up(sets):
        for l in range(2):
            sums = [jnp.sum(parts[s, l].astype(jnp.float32), axis=0) for s in range(sets)]
            out[l] = sum(sums) / (count - 1)

    @pl.when(outer)
    def _():
        pltpu.make_async_copy(parts.at[0], parts.at[0], r_recv).wait()
        add_up(1)

    @pl.when(jnp.logical_not(outer))
    def _():
        pltpu.make_async_copy(parts, parts, r_recv).wait()
        add_up(2)

    wait_blocks(3 * n_lon - 1, r_send)


def member_plan(members, gradient, lon_taper, lat_taper):
    n_lon, n_lat = lax.axis_size("lon"), lax.axis_size("lat")
    count, levels, clat, clon = members.shape
    share = count // n_lon
    frame = 3 * clat
    vmem = pl.BlockSpec(memory_space=pltpu.VMEM)
    hbm = pl.BlockSpec(memory_space=pl.ANY)
    dma = pltpu.SemaphoreType.DMA
    return pl.pallas_call(
        functools.partial(member_kernel, n_lon, n_lat, count),
        out_shape=pltpu.VMEM(gradient.shape, jnp.float32),
        in_specs=[hbm, hbm, hbm, hbm],
        out_specs=vmem,
        scratch_shapes=[
            pltpu.VMEM(lon_taper.shape, lon_taper.dtype),
            pltpu.VMEM(lat_taper.shape, lat_taper.dtype),
            pltpu.VMEM((3, levels, clat, clon), jnp.float32),
            pltpu.VMEM((n_lon, 3, clat, clon), jnp.float32),
            pltpu.VMEM((share, n_lon, frame, clon), jnp.bfloat16),
            pltpu.VMEM((n_lon // 2 * CHUNK * frame, 6 * clon), jnp.bfloat16),
            pltpu.VMEM((n_lon // 2 * CHUNK * frame, 2 * clon), jnp.bfloat16),
            pltpu.VMEM((n_lon // 2, frame, 2 * clon), jnp.float32),
            pltpu.VMEM((6 * clon, 2 * clon), jnp.bfloat16),
            pltpu.VMEM((frame, frame), jnp.bfloat16),
            pltpu.VMEM((n_lon, frame, clon), jnp.bfloat16),
            pltpu.VMEM((2, 2, n_lon, clat, clon), jnp.bfloat16),
            dma((2,)), dma((3,)), dma((3,)), dma, dma((n_lon,)), dma((n_lon,)),
            dma((share // CHUNK,)), dma((share // CHUNK,)), dma, dma,
        ],
        compiler_params=pltpu.CompilerParams(
            collective_id=0, has_side_effects=True, vmem_limit_bytes=VMEM_BYTES
        ),
    )(members, gradient, lon_taper, lat_taper)


def per_device(members, gradient, lon_taper, lat_taper):
    n_lon, n_lat = lax.axis_size("lon"), lax.axis_size("lat")
    count, levels, clat, clon = members.shape
    cycle = levels == 2 and n_lon % 2 == 0 and n_lon >= 6
    if cycle and n_lat == 4 and count % (n_lon * CHUNK) == 0 and count >= n_lon * n_lat * CHUNK:
        return member_plan(members, gradient, lon_taper, lat_taper)
    return halo_plan(members, gradient, lon_taper, lat_taper)


def solution(mesh):
    in_specs = (P(None, None, "lat", "lon"), P(None, "lat", "lon"), P(), P())
    out_specs = P(None, "lat", "lon")
    return jax.shard_map(
        per_device, mesh=mesh, in_specs=in_specs, out_specs=out_specs, check_vma=False
    )
```
